32 devices in a mesh: lev: 2 (over y), tile: 16 (over z, x, core).
Axes of the slice: x: 2, y: 2, z: 4, core: 2. Of those that a mesh axis runs over, the one named last changes fastest.
Arguments:
- prognostic: float32 [4, 128, 131072], P(None, 'lev', 'tile'), may hold values from -6 to 6
- neighbours: int32 [4, 131072], P(None, 'tile'), may hold values from 0 to 8447, as said below
- metric: float32 [2, 4, 131072], P(None, None, 'tile'), may hold values from -0.9 to 0.9
- inverses: float32 [16, 128, 128], P('tile')
Outputs:
- advanced: float32 [4, 128, 131072], P(None, 'lev', 'tile')
The draws below stay inside these ranges and needn't reach their ends.
Inputs may be any that keep to these rules, and one draw needn't show every extreme that they name: `neighbours`: entry [k, c] indexes the cells of c's tile extended by 128 cells on each side: 0 to 127 are the last 128 cells of the previous tile, then the tile's own 8192 cells in order, then the first 128 cells of the next tile, the tiles forming a closed cycle; each entry lies within 128 of 128 + (c mod 8192).
All inputs are finite; a program needn't handle non-finite values.
Results may differ from the reference program's by a relative error of at most 0.0001.
Values sent between devices are 32-bit elements; how exact they have to be, the bound alone decides.
No kernel may reach another device: no remote copies, remote signals or barrier semaphores. Data moves between devices by JAX's collectives and lax.ppermute only.
A program may use at most 128 MiB of HBM per device.

```python
import math
import jax
import jax.numpy as jnp
from jax import lax

NLEV = 128
CELLS_DEV = 8192
NB = 4
HALO = 128
SUBSTEPS = 3
CELLS = 131072
REGIONS = 16


def draw_neighbours(key, part):
    offsets = jax.random.randint(key, (NB, CELLS), -HALO, HALO + 1)
    position = jnp.arange(CELLS, dtype=jnp.int32) % CELLS_DEV
    local_index = HALO + position[None, :] + offsets
    first_row = jnp.arange(NB, dtype=jnp.int32)[:, None] == 0
    local_index = jnp.where(first_row & (position[None, :] == 0), 0, local_index)
    local_index = jnp.where(first_row & (position[None, :] == CELLS_DEV - 1), CELLS_DEV + 2 * HALO - 1, local_index)
    return local_index.astype(jnp.int32)


def draw_inverses(key, part):
    array_shape = (REGIONS, NLEV, NLEV)
    random_part = jnp.clip(jax.random.normal(key, array_shape, jnp.float32), -6.0, 6.0)
    row_index = lax.broadcasted_iota(jnp.int32, array_shape, 1)
    col_index = lax.broadcasted_iota(jnp.int32, array_shape, 2)
    diagonal = jnp.where(row_index == col_index, 1.0, 0.0).astype(jnp.float32)
    return diagonal + 0.25 / math.sqrt(NLEV) * random_part


def steps_of(own_key, shape, cuts, smallest, high):
    factor_of = 1.0
    for dim, shards_of in cuts:
        steps = jax.random.uniform(jax.random.fold_in(jax.random.fold_in(own_key, 6), dim), (shards_of,), jnp.float32, smallest / len(cuts), high / len(cuts))
        factor_of = factor_of * jnp.repeat(jnp.exp(steps), shape[dim] // shards_of).reshape((-1,) + (1,) * (len(shape) - 1 - dim))
    return factor_of


def noise(own_key, dims, scale, reach, shards=(), held_as=jnp.bfloat16):
    array = scale * jax.random.normal(own_key, dims, jnp.float32)
    if shards:
        array = array * steps_of(own_key, dims, shards, -0.22, 0.18)
    return jnp.clip(array, -reach, reach).astype(held_as)


def setup_inputs(seed: int = 0) -> dict:
    arg_keys = jax.random.split(jax.random.key(seed), 5)
    prognostic = noise(arg_keys[0], (4, NLEV, CELLS), 1.0, 6.0, ((1, 2), (2, 16)), jnp.float32)
    neighbours = draw_neighbours(jax.random.fold_in(arg_keys[4], 71), 0)
    metric = noise(arg_keys[2], (2, NB, CELLS), 0.15, 0.9, ((2, 16),), jnp.float32)
    inverses = draw_inverses(jax.random.fold_in(arg_keys[4], 71), 0)
    return dict(prognostic=prognostic, neighbours=neighbours, metric=metric, inverses=inverses)


acoustic = 0.4


def level_slope(padded):
    return 0.5 * (padded[2:] - padded[:-2])


def pad_levels(field):
    return jnp.pad(field, ((1, 1), (0, 0)))


def horizontal_step(moving, neighbours, metric):
    cell_count = moving.shape[2]
    position = jnp.arange(cell_count, dtype=jnp.int32)
    anchor = (position // CELLS_DEV) * CELLS_DEV - HALO
    gradient_east = jnp.zeros(moving.shape[1:], moving.dtype)
    gradient_north = jnp.zeros(moving.shape[1:], moving.dtype)
    diverge = jnp.zeros(moving.shape[1:], moving.dtype)
    for direction in range(NB):
        global_index = ((anchor + neighbours[direction]) % cell_count).astype(jnp.int32)
        nearby = jnp.take(moving, global_index, axis=2)
        change = nearby - moving
        weight_east = metric[0, direction]
        weight_north = metric[1, direction]
        gradient_east = gradient_east + weight_east * change[2]
        gradient_north = gradient_north + weight_north * change[2]
        diverge = diverge + (weight_east * change[0] + weight_north * change[1])
    return moving[0] - gradient_east, moving[1] - gradient_north, moving[2] - diverge


def reference(prognostic, neighbours, metric, inverses):
    fields = prognostic
    for substep in range(SUBSTEPS):
        east, north, pressure = horizontal_step(fields[:3], neighbours, metric)
        right_side = fields[3] - acoustic * level_slope(pad_levels(pressure))
        tiled = right_side.reshape(NLEV, REGIONS, CELLS_DEV)
        solved = jnp.einsum("tij,jtc->itc", inverses, tiled, precision=lax.Precision.HIGHEST)
        vertical = solved.reshape(NLEV, CELLS)
        pressure = pressure - acoustic * level_slope(pad_levels(vertical))
        fields = jnp.stack([east, north, pressure, vertical])
    return fields
```

```python
import functools

import jax
import jax.numpy as jnp
from jax import lax
from jax.experimental import pallas as pl
from jax.experimental.pallas import tpu as pltpu
from jax.sharding import PartitionSpec as P

HALO = 128
LANES = 128
BLOCK = 256
SUBSTEPS = 3
CHUNKS = 8
LAG = 3
EARLY = 3
UNROLL = 1
EDGE_LAG = 2
VMEM_LIMIT = 5 * 2**20

acoustic = 0.4
half_acoustic = 0.5 * acoustic

f32 = jnp.float32
bf16 = jnp.bfloat16


def dot(a, b):
    return jnp.dot(a, b, preferred_element_type=f32)


def exact_dot(a, b):
    return jnp.dot(a, b, preferred_element_type=f32, precision=lax.Precision.HIGHEST)


def split(x):
    hi = x.astype(bf16)
    return hi, (x - hi.astype(f32)).astype(bf16)


def aligned(x, to):
    return x if isinstance(x, int) else pl.multiple_of(x, to)


class Plan:
    def __init__(self, groups, levels, cells, directions):
        self.groups = groups
        self.levels = levels
        self.cells = cells
        self.directions = directions
        self.total = groups * levels
        self.chunks = CHUNKS
        self.width = cells // CHUNKS
        self.extras = 1 if groups == 2 else 2
        self.rows = -(-(self.total + self.extras * groups) // 16) * 16
        self.pieces = self.width // LANES
        self.sent = (levels + self.extras) * self.pieces
        self.slots = self.schedule()

    def schedule(self):
        chunks = self.chunks
        slots = [(0, (1 + q) % chunks) for q in range(chunks)]
        for substep in range(1, SUBSTEPS):
            done = {c: t + LAG for t, (s, c) in enumerate(slots) if s == substep - 1}
            ready = {}
            for c in range(chunks):
                at_edge = c in (0, chunks - 1)
                near = [done[d % chunks] + (EDGE_LAG if at_edge and not 0 <= d < chunks else 0) for d in (c - 1, c, c + 1)]
                ready[c] = (max(near), not at_edge)
            left = set(range(chunks))
            while left:
                now = [c for c in left if ready[c][0] <= len(slots)] or left
                c = min(now, key=lambda c: (ready[c][1], ready[c][0], c) if now is not left else (ready[c][0], c))
                left.remove(c)
                slots.append((substep, c))
        return slots


def operator(plan, me, inverse_ref, g_ref):
    levels, total, groups, rows = plan.levels, plan.total, plan.groups, plan.rows
    extras = plan.extras
    r = lax.broadcasted_iota(jnp.int32, (rows, total), 0)
    c = lax.broadcasted_iota(jnp.int32, (rows, total), 1)

    def wrapped(x):
        return jnp.where(x >= groups, x - groups, x)

    wanted = jnp.full((rows, total), -1, jnp.int32)
    for shift in range(groups):
        to = wrapped(me + shift)
        wanted = jnp.where((r >= shift * levels) & (r < (shift + 1) * levels), r - shift * levels + to * levels, wanted)
        first = total + shift * extras
        if groups == 2:
            edge = jnp.where(to == 0, levels, levels - 1)
            wanted = jnp.where(r == first, edge, wanted)
        else:
            wanted = jnp.where(r == first, to * levels - 1, wanted)
            wanted = jnp.where(r == first + 1, (to + 1) * levels, wanted)
    pick = (wanted == c).astype(f32)
    row = lax.broadcasted_iota(jnp.int32, (total, 2 * levels), 0)
    col = lax.broadcasted_iota(jnp.int32, (total, 2 * levels), 1)
    own = me * levels + jnp.where(col >= levels, col - levels, col)
    slope = jnp.where(row == own - 1, -half_acoustic, 0.0) + jnp.where(row == own + 1, half_acoustic, 0.0)
    mix = jnp.where(col < levels, jnp.where(row == own, 1.0, 0.0), slope)
    g = exact_dot(exact_dot(pick, inverse_ref[...]), mix)
    hi, lo = split(g)
    g_ref[0:rows, :] = hi
    g_ref[rows : 2 * rows, :] = lo


def correct(plan, me, fields, x_ref, chunk, got):
    levels, pieces = plan.levels, plan.pieces
    row = lax.broadcasted_iota(jnp.int32, (levels, LANES), 0)
    for j in range(pieces):
        cols = pl.ds(chunk * plan.width + j * LANES, LANES)
        v = fields[3, :, cols]
        for g in got:
            v = v + g[j * levels : (j + 1) * levels, :]
        x = []
        for e in range(plan.extras):
            at = levels * pieces + e * pieces + j
            one = x_ref[e : e + 1, cols]
            for g in got:
                one = one + g[at : at + 1, :]
            x.append(one)
        if plan.groups == 2:
            below = jnp.where(me == 0, 0.0, x[0])
            above = jnp.where(me == 0, x[0], 0.0)
        else:
            below, above = x
        down = jnp.where(row == 0, below, pltpu.roll(v, 1, 0))
        up = jnp.where(row == levels - 1, above, pltpu.roll(v, levels - 1, 0))
        fields[2, :, cols] = fields[2, :, cols] - half_acoustic * (up - down)
        fields[3, :, cols] = v


def weights(plan, start, first, near_ref, metric_ref, m_ref, sum_ref):
    span = BLOCK + 2 * HALO
    piece = 32
    cols = pl.ds(first, BLOCK)
    local = [near_ref[k : k + 1, cols] - (start + first) for k in range(plan.directions)]
    east = [metric_ref[0, k : k + 1, cols] for k in range(plan.directions)]
    north = [metric_ref[1, k : k + 1, cols] for k in range(plan.directions)]
    sum_ref[0:1, cols] = functools.reduce(jnp.add, east)
    sum_ref[1:2, cols] = functools.reduce(jnp.add, north)
    for r in range(0, span, piece):
        slot = lax.broadcasted_iota(jnp.int32, (piece, BLOCK), 0) + r
        e = n = None
        for k in range(plan.directions):
            hit = slot == local[k]
            ek = jnp.where(hit, east[k], 0.0)
            nk = jnp.where(hit, north[k], 0.0)
            e = ek if e is None else e + ek
            n = nk if n is None else n + nk
        here = slice(r, r + piece)
        m_ref[0, here, :], m_ref[1, here, :] = split(e)
        m_ref[2, here, :], m_ref[3, here, :] = split(n)


def advance(plan, pieces, src, origin, new, start, m, build, sum_ref, g_ref, f, x_ref, sends):
    levels, width = plan.levels, plan.width
    span = BLOCK + 2 * HALO
    blocks = width // BLOCK
    for ref, col, into, count in pieces:
        there = pl.ds(into, count)
        for field, places in ((0, ((1,), (0,))), (1, ((6,), (7,))), (2, ((2, 5), (3, 4)))):
            for part, rows in zip(split(ref[field, :, pl.ds(col, count)]), places):
                for at in rows:
                    f[at * levels : (at + 1) * levels, there] = part

    def block(b, carry):
        first = aligned(b * BLOCK, BLOCK)
        if build is not None:
            build(first, m.at[b])
        cols = pl.ds(first, BLOCK)
        mine = pl.ds(aligned(origin + first, LANES), BLOCK)
        into = pl.ds(aligned(start + first, BLOCK), BLOCK)
        wide = pl.ds(first, span)
        eh = dot(f[0 : 4 * levels, wide], m[b, 0])
        el = dot(f[levels : 3 * levels, wide], m[b, 1])
        nh = dot(f[4 * levels : 8 * levels, wide], m[b, 2])
        nl = dot(f[5 * levels : 7 * levels, wide], m[b, 3])

        def rows(x, i):
            return x[i * levels : (i + 1) * levels]

        ue = rows(eh, 0) + rows(eh, 1) + rows(el, 0)
        pe = rows(eh, 2) + rows(eh, 3) + rows(el, 1)
        pn = rows(nh, 0) + rows(nh, 1) + rows(nl, 0)
        vn = rows(nh, 2) + rows(nh, 3) + rows(nl, 1)
        se, sn = sum_ref[0:1, cols], sum_ref[1:2, cols]
        u, v, p = src[0, :, mine], src[1, :, mine], src[2, :, mine]
        new[0, :, into] = u - (pe - se * p)
        new[1, :, into] = v - (pn - sn * p)
        pressure = p - ((ue - se * u) + (vn - sn * v))
        new[2, :, into] = pressure
        z_hi, z_lo = split(jnp.concatenate([src[3, :, mine], pressure], axis=0))
        y2 = dot(g_ref[...], z_hi)
        y = y2[: plan.rows] + y2[plan.rows :] + dot(g_ref[0 : plan.rows, :], z_lo)
        new[3, :, into] = y[:levels]
        x_ref[:, into] = y[plan.total : plan.total + 8]
        for s, send in enumerate(sends):
            for i in range(BLOCK // LANES):
                part = slice(i * LANES, (i + 1) * LANES)
                j = b * (BLOCK // LANES) + i
                send[pl.ds(aligned(j * levels, 8), levels), :] = y[(s + 1) * levels : (s + 2) * levels, part]
                for e in range(plan.extras):
                    at = plan.total + (s + 1) * plan.extras + e
                    send[pl.ds(levels * plan.pieces + e * plan.pieces + j, 1), :] = y[at : at + 1, part]
        return carry

    if build is None:
        lax.fori_loop(0, blocks, block, 0, unroll=UNROLL)
    else:
        for b in range(blocks):
            block(b, 0)


FAR = ("prognostic", "inverse", "near", "metric", "result")


def call(plan, arrays, outs, aliased, chunk=None, fixes=(), setup=False):
    groups, levels, cells, width, chunks = plan.groups, plan.levels, plan.cells, plan.width, plan.chunks
    in_names, out_names = list(arrays), list(outs)
    fresh = "prognostic" in arrays

    scratch = {}
    if chunk is not None:
        scratch["f"] = pltpu.VMEM((8 * levels, width + 2 * HALO), bf16)
    if fresh:
        scratch["win"] = pltpu.VMEM((4, levels, width + 2 * HALO), f32)
        scratch["near_v"] = pltpu.VMEM((plan.directions, width), jnp.int32)
        scratch["met_v"] = pltpu.VMEM((2, plan.directions, width), f32)
    if setup:
        scratch["inv_v"] = pltpu.VMEM((plan.total, plan.total), f32)
    scratch["sems"] = pltpu.SemaphoreType.DMA((8,))
    scratch_names = list(scratch)

    def kernel(*refs):
        r = dict(zip(in_names, refs))
        r.update(zip(out_names, refs[len(in_names) :]))
        r.update(zip(scratch_names, refs[len(in_names) + len(out_names) :]))
        used = [0]

        def copy(src, dst):
            c = pltpu.make_async_copy(src, dst, r["sems"].at[used[0]])
            used[0] += 1
            c.start()
            return c

        who = r["me"][0]
        stores = []
        if fresh:
            start = chunk * width
            lo = start if chunk == 0 else start - HALO
            hi = start + width if chunk == chunks - 1 else start + width + HALO
            into = lo - (start - HALO)
            near = pl.ds(start, width)
            loads = [copy(r["near"].at[:, near], r["near_v"]), copy(r["metric"].at[:, :, near], r["met_v"])]
            if setup:
                loads.append(copy(r["inverse"], r["inv_v"]))
            late = copy(r["prognostic"].at[:, :, pl.ds(lo, hi - lo)], r["win"].at[:, :, pl.ds(into, hi - lo)])
            for c in loads:
                c.wait()
            if setup:
                operator(plan, who, r["inv_v"], r["g"])
            late.wait()
        for name, b in fixes:
            at = pl.ds(b * width, width)
            got = [r[f"got_{name}{b}_{s}"] for s in range(groups - 1)]
            if "result" in r:
                stores.append(copy(r[name].at[0:2, :, at], r["result"].at[0:2, :, at]))
            correct(plan, who, r[name], r[f"{name}_x"], b, got)
            if "result" in r:
                stores.append(copy(r[name].at[2:4, :, at], r["result"].at[2:4, :, at]))
            if b == 0 and "edge_low" in r:
                r["edge_low"][...] = r[name][0:3, :, 0:HALO]
            if b == chunks - 1 and "edge_high" in r:
                r["edge_high"][...] = r[name][0:3, :, cells - HALO : cells]
        if chunk is not None:
            start = chunk * width
            src, origin = (r["win"], HALO) if fresh else (r["old"], start)
            lo = origin if chunk == 0 else origin - HALO
            hi = origin + width if chunk == chunks - 1 else origin + width + HALO
            pieces = [(src, lo, lo - (origin - HALO), hi - lo)]
            if chunk == 0:
                pieces.append((r["halo_low"], 0, 0, HALO))
            if chunk == chunks - 1:
                pieces.append((r["halo_high"], 0, width + HALO, HALO))
            sends = [r[f"send{s}"] for s in range(groups - 1)]
            build = None
            if fresh:

                def build(first, m):
                    weights(plan, start, first, r["near_v"], r["met_v"], m, r["sums"])

            advance(
                plan, pieces, src, origin, r["new"], start, r["m"], build, r["sums"], r["g"], r["f"], r["new_x"], sends
            )
        for c in stores:
            c.wait()

    def spec(name):
        if name == "me":
            return pl.BlockSpec(memory_space=pltpu.SMEM)
        return pl.BlockSpec(memory_space=pltpu.HBM if name in FAR else pltpu.VMEM)

    def shape(name):
        s = outs[name]
        return (pltpu.HBM if name in FAR else pltpu.VMEM)(s.shape, s.dtype)

    def placed(name, x):
        if name == "me":
            return x
        return pltpu.with_memory_space_constraint(x, pltpu.HBM if name in FAR else pltpu.VMEM)

    results = pl.pallas_call(
        kernel,
        out_shape=[shape(name) for name in out_names],
        in_specs=[spec(name) for name in in_names],
        out_specs=[spec(name) for name in out_names],
        scratch_shapes=list(scratch.values()),
        input_output_aliases={in_names.index(name): out_names.index(name) for name in aliased},
        cost_estimate=pl.CostEstimate(flops=0, bytes_accessed=0, transcendentals=0),
        compiler_params=pltpu.CompilerParams(vmem_limit_bytes=VMEM_LIMIT),
        name=f"advance_{chunk}" if chunk is not None else "complete",
    )(*[placed(name, x) for name, x in arrays.items()])
    return dict(zip(out_names, results))


def per_device(prognostic, neighbours, metric, inverses):
    groups = lax.axis_size("lev")
    tiles = lax.axis_size("tile")
    levels, cells = prognostic.shape[1:]
    plan = Plan(groups, levels, cells, neighbours.shape[0])
    me = lax.axis_index("lev").astype(jnp.int32).reshape(1)

    def shape(dims, dtype=f32):
        return jax.ShapeDtypeStruct(dims, dtype)

    def shifted(x, by):
        return lax.ppermute(x, "lev", [(i, (i + by) % groups) for i in range(groups)])

    def from_low(x):
        return lax.ppermute(x, "tile", [(i, (i + 1) % tiles) for i in range(tiles)])

    def from_high(x):
        return lax.ppermute(x, "tile", [((i + 1) % tiles, i) for i in range(tiles)])

    halo_low = from_low(prognostic[0:3, :, cells - HALO :])
    halo_high = from_high(prognostic[0:3, :, :HALO])
    last = plan.chunks - 1
    state = {}
    kept, got = {}, {}
    g = result = None
    fixed = set()
    for slot in range(len(plan.slots) + LAG):
        substep, chunk = plan.slots[slot] if slot < len(plan.slots) else (SUBSTEPS - 1, None)
        due = [x for x in plan.slots[: max(slot - LAG + 1, 0)] if x not in fixed]
        if chunk is not None and substep > 0:
            due += [(substep - 1, c) for c in (chunk - 1, chunk, chunk + 1) if 0 <= c <= last and (substep - 1, c) not in fixed]
        due = list(dict.fromkeys(due))
        fixed.update(due)
        names = {substep: "new", substep - 1: "old"}
        arrays, outs, aliased = dict(me=me), {}, []
        for s in sorted({x[0] for x in due} | ({substep, substep - 1} if chunk is not None else set())):
            if s < 0:
                continue
            name = names[s]
            written = s == substep and chunk is not None
            if s in state:
                arrays[name], arrays[f"{name}_x"] = state[s]
            if written or any(x[0] == s for x in due):
                outs[name] = shape(prognostic.shape)
                if s in state:
                    aliased.append(name)
            if written:
                outs[f"{name}_x"] = shape((8, cells))
                if s in state:
                    aliased.append(f"{name}_x")
        for x in due:
            for i in range(groups - 1):
                arrays[f"got_{names[x[0]]}{x[1]}_{i}"] = got[x][i]
            if x[0] < SUBSTEPS - 1 and x[1] in (0, last):
                outs["edge_low" if x[1] == 0 else "edge_high"] = shape((3, levels, HALO))
            if x[0] == SUBSTEPS - 1 and "result" not in outs:
                outs["result"] = shape(prognostic.shape)
                if result is not None:
                    arrays["result"] = result
                    aliased.append("result")
        setup = g is None
        if chunk is not None:
            if substep == 0:
                arrays.update(prognostic=prognostic, near=neighbours, metric=metric)
                outs["m"] = shape((plan.width // BLOCK, 4, BLOCK + 2 * HALO, BLOCK), dtype=bf16)
                outs["sums"] = shape((8, plan.width))
            else:
                arrays.update(m=kept[chunk][0], sums=kept[chunk][1])
            early = slot == EARLY
            if chunk == 0 or early:
                arrays["halo_low"] = halo_low
            if chunk == last or early:
                arrays["halo_high"] = halo_high
            if setup:
                arrays["inverse"] = inverses[0]
                outs["g"] = shape((2 * plan.rows, 2 * levels), dtype=bf16)
            else:
                arrays["g"] = g
            for i in range(groups - 1):
                outs[f"send{i}"] = shape((plan.sent, LANES))
        fixes = [(names[s], c) for s, c in due]
        res = call(plan, arrays, outs, aliased, chunk=chunk, fixes=fixes, setup=setup)
        g = res.get("g", g)
        result = res.get("result", result)
        for s, name in names.items():
            if name in res:
                state[s] = res[name], res.get(f"{name}_x", state[s][1] if s in state else None)
        if chunk is not None:
            if substep == 0:
                kept[chunk] = res["m"], res["sums"]
            got[substep, chunk] = [shifted(res[f"send{i}"], i + 1) for i in range(groups - 1)]
        if "edge_high" in res:
            halo_low = from_low(res["edge_high"])
        if "edge_low" in res:
            halo_high = from_high(res["edge_low"])
    return result


def solution(mesh):
    in_specs = (
        P(None, "lev", "tile"),
        P(None, "tile"),
        P(None, None, "tile"),
        P("tile", None, None),
    )
    out_specs = P(None, "lev", "tile")
    return jax.shard_map(
        per_device, mesh=mesh, in_specs=in_specs, out_specs=out_specs, check_vma=False
    )
```

```python
import functools

import jax
import jax.numpy as jnp
from jax import lax
from jax.experimental import pallas as pl
from jax.experimental.pallas import tpu as pltpu
from jax.sharding import PartitionSpec as P

HALO = 128
LANES = 128
BLOCK = 256
SUBSTEPS = 3
CHUNKS = 8
LAG = 4
EARLY = 6
UNROLL = 1
EDGE_LAG = 2
VMEM_LIMIT = 5 * 2**20

acoustic = 0.4
half_acoustic = 0.5 * acoustic

f32 = jnp.float32
bf16 = jnp.bfloat16


def dot(a, b):
    return jnp.dot(a, b, preferred_element_type=f32)


def exact_dot(a, b):
    return jnp.dot(a, b, preferred_element_type=f32, precision=lax.Precision.HIGHEST)


def split(x):
    hi = x.astype(bf16)
    return hi, (x - hi.astype(f32)).astype(bf16)


def aligned(x, to):
    return x if isinstance(x, int) else pl.multiple_of(x, to)


class Plan:
    def __init__(self, groups, levels, cells, directions):
        self.groups = groups
        self.levels = levels
        self.cells = cells
        self.directions = directions
        self.total = groups * levels
        self.chunks = CHUNKS
        self.width = cells // CHUNKS
        self.extras = 1 if groups == 2 else 2
        self.rows = -(-(self.total + self.extras * groups) // 16) * 16
        self.pieces = self.width // LANES
        self.sent = (levels + self.extras) * self.pieces
        self.slots = self.schedule()

    def schedule(self):
        chunks = self.chunks
        slots = [(0, (1 + q) % chunks) for q in range(chunks)]
        for substep in range(1, SUBSTEPS):
            done = {c: t + LAG for t, (s, c) in enumerate(slots) if s == substep - 1}
            ready = {}
            for c in range(chunks):
                at_edge = c in (0, chunks - 1)
                near = [done[d % chunks] + (EDGE_LAG if at_edge and not 0 <= d < chunks else 0) for d in (c - 1, c, c + 1)]
                ready[c] = (max(near), not at_edge)
            left = set(range(chunks))
            while left:
                now = [c for c in left if ready[c][0] <= len(slots)] or left
                c = min(now, key=lambda c: (ready[c][1], ready[c][0], c) if now is not left else (ready[c][0], c))
                left.remove(c)
                slots.append((substep, c))
        return slots


def operator(plan, me, inverse_ref, g_ref):
    levels, total, groups, rows = plan.levels, plan.total, plan.groups, plan.rows
    extras = plan.extras
    r = lax.broadcasted_iota(jnp.int32, (rows, total), 0)
    c = lax.broadcasted_iota(jnp.int32, (rows, total), 1)

    def wrapped(x):
        return jnp.where(x >= groups, x - groups, x)

    wanted = jnp.full((rows, total), -1, jnp.int32)
    for shift in range(groups):
        to = wrapped(me + shift)
        wanted = jnp.where((r >= shift * levels) & (r < (shift + 1) * levels), r - shift * levels + to * levels, wanted)
        first = total + shift * extras
        if groups == 2:
            edge = jnp.where(to == 0, levels, levels - 1)
            wanted = jnp.where(r == first, edge, wanted)
        else:
            wanted = jnp.where(r == first, to * levels - 1, wanted)
            wanted = jnp.where(r == first + 1, (to + 1) * levels, wanted)
    pick = (wanted == c).astype(f32)
    row = lax.broadcasted_iota(jnp.int32, (total, 2 * levels), 0)
    col = lax.broadcasted_iota(jnp.int32, (total, 2 * levels), 1)
    own = me * levels + jnp.where(col >= levels, col - levels, col)
    slope = jnp.where(row == own - 1, -half_acoustic, 0.0) + jnp.where(row == own + 1, half_acoustic, 0.0)
    mix = jnp.where(col < levels, jnp.where(row == own, 1.0, 0.0), slope)
    g = exact_dot(exact_dot(pick, inverse_ref[...]), mix)
    hi, lo = split(g)
    g_ref[0:rows, :] = hi
    g_ref[rows : 2 * rows, :] = lo


def correct(plan, me, fields, x_ref, chunk, got):
    levels, pieces = plan.levels, plan.pieces
    row = lax.broadcasted_iota(jnp.int32, (levels, LANES), 0)
    for j in range(pieces):
        cols = pl.ds(chunk * plan.width + j * LANES, LANES)
        v = fields[3, :, cols]
        for g in got:
            v = v + g[j * levels : (j + 1) * levels, :]
        x = []
        for e in range(plan.extras):
            at = levels * pieces + e * pieces + j
            one = x_ref[e : e + 1, cols]
            for g in got:
                one = one + g[at : at + 1, :]
            x.append(one)
        if plan.groups == 2:
            below = jnp.where(me == 0, 0.0, x[0])
            above = jnp.where(me == 0, x[0], 0.0)
        else:
            below, above = x
        down = jnp.where(row == 0, below, pltpu.roll(v, 1, 0))
        up = jnp.where(row == levels - 1, above, pltpu.roll(v, levels - 1, 0))
        fields[2, :, cols] = fields[2, :, cols] - half_acoustic * (up - down)
        fields[3, :, cols] = v


def weights(plan, start, first, near_ref, metric_ref, m_ref, sum_ref):
    span = BLOCK + 2 * HALO
    tall = 16
    cols = pl.ds(first, BLOCK)
    directions = range(plan.directions)
    local = [near_ref[k : k + 1, cols] - (start + first) for k in directions]
    index = [jnp.broadcast_to(x, (tall, BLOCK)).astype(jnp.int16) for x in local]
    parts = []
    for which in range(2):
        w = [metric_ref[which, k : k + 1, cols] for k in directions]
        sum_ref[which : which + 1, cols] = functools.reduce(jnp.add, w)
        joined = []
        for k in directions:
            x = w[k]
            for j in range(k + 1, plan.directions):
                x = x + jnp.where(local[j] == local[k], w[j], 0.0)
            joined.append(jnp.broadcast_to(x, (tall, BLOCK)))
        pairs = [split(x) for x in joined]
        parts.append([p[0] for p in pairs])
        parts.append([p[1] for p in pairs])
    row = lax.broadcasted_iota(jnp.int32, (tall, BLOCK), 0).astype(jnp.int16)
    zero = jnp.zeros((tall, BLOCK), bf16)
    for r in range(0, span, tall):
        slot = row + jnp.int16(r)
        hits = [slot == index[k] for k in directions]
        for i, values in enumerate(parts):
            x = zero
            for k in reversed(directions):
                x = jnp.where(hits[k], values[k], x)
            m_ref[i, r : r + tall, :] = x


def advance(plan, pieces, src, origin, new, start, m, build, sum_ref, g_ref, f, x_ref, sends):
    levels, width = plan.levels, plan.width
    span = BLOCK + 2 * HALO
    blocks = width // BLOCK
    for ref, col, into, count in pieces:
        there = pl.ds(into, count)
        for field, places in ((0, ((1,), (0,))), (1, ((6,), (7,))), (2, ((2, 5), (3, 4)))):
            for part, rows in zip(split(ref[field, :, pl.ds(col, count)]), places):
                for at in rows:
                    f[at * levels : (at + 1) * levels, there] = part

    def block(b, carry):
        first = aligned(b * BLOCK, BLOCK)
        if build is not None and b > 0:
            build(first, m.at[b])
        cols = pl.ds(first, BLOCK)
        mine = pl.ds(aligned(origin + first, LANES), BLOCK)
        into = pl.ds(aligned(start + first, BLOCK), BLOCK)
        wide = pl.ds(first, span)
        eh = dot(f[0 : 4 * levels, wide], m[b, 0])
        el = dot(f[levels : 3 * levels, wide], m[b, 1])
        nh = dot(f[4 * levels : 8 * levels, wide], m[b, 2])
        nl = dot(f[5 * levels : 7 * levels, wide], m[b, 3])

        def rows(x, i):
            return x[i * levels : (i + 1) * levels]

        ue = rows(eh, 0) + rows(eh, 1) + rows(el, 0)
        pe = rows(eh, 2) + rows(eh, 3) + rows(el, 1)
        pn = rows(nh, 0) + rows(nh, 1) + rows(nl, 0)
        vn = rows(nh, 2) + rows(nh, 3) + rows(nl, 1)
        se, sn = sum_ref[0:1, cols], sum_ref[1:2, cols]
        u, v, p = src[0, :, mine], src[1, :, mine], src[2, :, mine]
        new[0, :, into] = u - (pe - se * p)
        new[1, :, into] = v - (pn - sn * p)
        pressure = p - ((ue - se * u) + (vn - sn * v))
        new[2, :, into] = pressure
        z_hi, z_lo = split(jnp.concatenate([src[3, :, mine], pressure], axis=0))
        y2 = dot(g_ref[...], z_hi)
        y = y2[: plan.rows] + y2[plan.rows :] + dot(g_ref[0 : plan.rows, :], z_lo)
        new[3, :, into] = y[:levels]
        x_ref[:, into] = y[plan.total : plan.total + 8]
        for s, send in enumerate(sends):
            for i in range(BLOCK // LANES):
                part = slice(i * LANES, (i + 1) * LANES)
                j = b * (BLOCK // LANES) + i
                send[pl.ds(aligned(j * levels, 8), levels), :] = y[(s + 1) * levels : (s + 2) * levels, part]
                for e in range(plan.extras):
                    at = plan.total + (s + 1) * plan.extras + e
                    send[pl.ds(levels * plan.pieces + e * plan.pieces + j, 1), :] = y[at : at + 1, part]
        return carry

    if build is None:
        lax.fori_loop(0, blocks, block, 0, unroll=UNROLL)
    else:
        for b in range(blocks):
            block(b, 0)


FAR = ("prognostic", "inverse", "near", "metric", "result")


def call(plan, arrays, outs, aliased, chunk=None, fixes=(), setup=False):
    groups, levels, cells, width, chunks = plan.groups, plan.levels, plan.cells, plan.width, plan.chunks
    in_names, out_names = list(arrays), list(outs)
    fresh = "prognostic" in arrays

    scratch = {}
    if chunk is not None:
        scratch["f"] = pltpu.VMEM((8 * levels, width + 2 * HALO), bf16)
    if fresh:
        scratch["win"] = pltpu.VMEM((4, levels, width + 2 * HALO), f32)
        scratch["near_v"] = pltpu.VMEM((plan.directions, width), jnp.int32)
        scratch["met_v"] = pltpu.VMEM((2, plan.directions, width), f32)
    if setup:
        scratch["inv_v"] = pltpu.VMEM((plan.total, plan.total), f32)
    scratch["sems"] = pltpu.SemaphoreType.DMA((8,))
    scratch_names = list(scratch)

    def kernel(*refs):
        r = dict(zip(in_names, refs))
        r.update(zip(out_names, refs[len(in_names) :]))
        r.update(zip(scratch_names, refs[len(in_names) + len(out_names) :]))
        used = [0]

        def copy(src, dst):
            c = pltpu.make_async_copy(src, dst, r["sems"].at[used[0]])
            used[0] += 1
            c.start()
            return c

        who = r["me"][0]
        stores = []
        if fresh:
            start = chunk * width
            lo = start if chunk == 0 else start - HALO
            hi = start + width if chunk == chunks - 1 else start + width + HALO
            into = lo - (start - HALO)
            near = pl.ds(start, width)
            loads = [copy(r["near"].at[:, near], r["near_v"]), copy(r["metric"].at[:, :, near], r["met_v"])]
            if setup:
                loads.append(copy(r["inverse"], r["inv_v"]))
            late = copy(r["prognostic"].at[:, :, pl.ds(lo, hi - lo)], r["win"].at[:, :, pl.ds(into, hi - lo)])
            for c in loads:
                c.wait()
            if setup:
                operator(plan, who, r["inv_v"], r["g"])
        for name, b in fixes:
            at = pl.ds(b * width, width)
            got = [r[f"got_{name}{b}_{s}"] for s in range(groups - 1)]
            if "result" in r:
                stores.append(copy(r[name].at[0:2, :, at], r["result"].at[0:2, :, at]))
            correct(plan, who, r[name], r[f"{name}_x"], b, got)
            if "result" in r:
                stores.append(copy(r[name].at[2:4, :, at], r["result"].at[2:4, :, at]))
            if b == 0 and "edge_low" in r:
                r["edge_low"][...] = r[name][0:3, :, 0:HALO]
            if b == chunks - 1 and "edge_high" in r:
                r["edge_high"][...] = r[name][0:3, :, cells - HALO : cells]
        if chunk is not None:
            start = chunk * width
            src, origin = (r["win"], HALO) if fresh else (r["old"], start)
            lo = origin if chunk == 0 else origin - HALO
            hi = origin + width if chunk == chunks - 1 else origin + width + HALO
            pieces = [(src, lo, lo - (origin - HALO), hi - lo)]
            if chunk == 0:
                pieces.append((r["halo_low"], 0, 0, HALO))
            if chunk == chunks - 1:
                pieces.append((r["halo_high"], 0, width + HALO, HALO))
            sends = [r[f"send{s}"] for s in range(groups - 1)]
            build = None
            if fresh:

                def build(first, m):
                    weights(plan, start, first, r["near_v"], r["met_v"], m, r["sums"])

            if fresh:
                build(0, r["m"].at[0])
                late.wait()
            advance(
                plan, pieces, src, origin, r["new"], start, r["m"], build, r["sums"], r["g"], r["f"], r["new_x"], sends
            )
        for c in stores:
            c.wait()

    def spec(name):
        if name == "me":
            return pl.BlockSpec(memory_space=pltpu.SMEM)
        return pl.BlockSpec(memory_space=pltpu.HBM if name in FAR else pltpu.VMEM)

    def shape(name):
        s = outs[name]
        return (pltpu.HBM if name in FAR else pltpu.VMEM)(s.shape, s.dtype)

    def placed(name, x):
        if name == "me":
            return x
        return pltpu.with_memory_space_constraint(x, pltpu.HBM if name in FAR else pltpu.VMEM)

    results = pl.pallas_call(
        kernel,
        out_shape=[shape(name) for name in out_names],
        in_specs=[spec(name) for name in in_names],
        out_specs=[spec(name) for name in out_names],
        scratch_shapes=list(scratch.values()),
        input_output_aliases={in_names.index(name): out_names.index(name) for name in aliased},
        cost_estimate=pl.CostEstimate(flops=0, bytes_accessed=0, transcendentals=0),
        compiler_params=pltpu.CompilerParams(vmem_limit_bytes=VMEM_LIMIT),
        name=f"advance_{chunk}" if chunk is not None else "complete",
    )(*[placed(name, x) for name, x in arrays.items()])
    return dict(zip(out_names, results))


def per_device(prognostic, neighbours, metric, inverses):
    groups = lax.axis_size("lev")
    tiles = lax.axis_size("tile")
    levels, cells = prognostic.shape[1:]
    plan = Plan(groups, levels, cells, neighbours.shape[0])
    me = lax.axis_index("lev").astype(jnp.int32).reshape(1)

    def shape(dims, dtype=f32):
        return jax.ShapeDtypeStruct(dims, dtype)

    def shifted(x, by):
        return lax.ppermute(x, "lev", [(i, (i + by) % groups) for i in range(groups)])

    def from_low(x):
        return lax.ppermute(x, "tile", [(i, (i + 1) % tiles) for i in range(tiles)])

    def from_high(x):
        return lax.ppermute(x, "tile", [((i + 1) % tiles, i) for i in range(tiles)])

    halo_low = from_low(prognostic[0:3, :, cells - HALO :])
    halo_high = from_high(prognostic[0:3, :, :HALO])
    last = plan.chunks - 1
    state = {}
    kept, got = {}, {}
    g = result = None
    fixed = set()
    for slot in range(len(plan.slots) + LAG):
        substep, chunk = plan.slots[slot] if slot < len(plan.slots) else (SUBSTEPS - 1, None)
        due = [x for x in plan.slots[: max(slot - LAG + 1, 0)] if x not in fixed]
        if chunk is not None and substep > 0:
            due += [(substep - 1, c) for c in (chunk - 1, chunk, chunk + 1) if 0 <= c <= last and (substep - 1, c) not in fixed]
        due = list(dict.fromkeys(due))
        fixed.update(due)
        names = {substep: "new", substep - 1: "old"}
        arrays, outs, aliased = dict(me=me), {}, []
        for s in sorted({x[0] for x in due} | ({substep, substep - 1} if chunk is not None else set())):
            if s < 0:
                continue
            name = names[s]
            written = s == substep and chunk is not None
            if s in state:
                arrays[name], arrays[f"{name}_x"] = state[s]
            if written or any(x[0] == s for x in due):
                outs[name] = shape(prognostic.shape)
                if s in state:
                    aliased.append(name)
            if written:
                outs[f"{name}_x"] = shape((8, cells))
                if s in state:
                    aliased.append(f"{name}_x")
        for x in due:
            for i in range(groups - 1):
                arrays[f"got_{names[x[0]]}{x[1]}_{i}"] = got[x][i]
            if x[0] < SUBSTEPS - 1 and x[1] in (0, last):
                outs["edge_low" if x[1] == 0 else "edge_high"] = shape((3, levels, HALO))
            if x[0] == SUBSTEPS - 1 and "result" not in outs:
                outs["result"] = shape(prognostic.shape)
                if result is not None:
                    arrays["result"] = result
                    aliased.append("result")
        setup = g is None
        if chunk is not None:
            if substep == 0:
                arrays.update(prognostic=prognostic, near=neighbours, metric=metric)
                outs["m"] = shape((plan.width // BLOCK, 4, BLOCK + 2 * HALO, BLOCK), dtype=bf16)
                outs["sums"] = shape((8, plan.width))
            else:
                arrays.update(m=kept[chunk][0], sums=kept[chunk][1])
            early = slot == EARLY
            if chunk == 0 or early:
                arrays["halo_low"] = halo_low
            if chunk == last or early:
                arrays["halo_high"] = halo_high
            if setup:
                arrays["inverse"] = inverses[0]
                outs["g"] = shape((2 * plan.rows, 2 * levels), dtype=bf16)
            else:
                arrays["g"] = g
            for i in range(groups - 1):
                outs[f"send{i}"] = shape((plan.sent, LANES))
        fixes = [(names[s], c) for s, c in due]
        res = call(plan, arrays, outs, aliased, chunk=chunk, fixes=fixes, setup=setup)
        g = res.get("g", g)
        result = res.get("result", result)
        for s, name in names.items():
            if name in res:
                state[s] = res[name], res.get(f"{name}_x", state[s][1] if s in state else None)
        if chunk is not None:
            if substep == 0:
                kept[chunk] = res["m"], res["sums"]
            got[substep, chunk] = [shifted(res[f"send{i}"], i + 1) for i in range(groups - 1)]
        if "edge_high" in res:
            halo_low = from_low(res["edge_high"])
        if "edge_low" in res:
            halo_high = from_high(res["edge_low"])
    return result


def solution(mesh):
    in_specs = (
        P(None, "lev", "tile"),
        P(None, "tile"),
        P(None, None, "tile"),
        P("tile", None, None),
    )
    out_specs = P(None, "lev", "tile")
    return jax.shard_map(
        per_device, mesh=mesh, in_specs=in_specs, out_specs=out_specs, check_vma=False
    )
```

```python
import functools

import jax
import jax.numpy as jnp
from jax import lax
from jax.experimental import pallas as pl
from jax.experimental.pallas import tpu as pltpu
from jax.sharding import PartitionSpec as P

HALO = 128
LANES = 128
BLOCK = 256
SUBSTEPS = 3
SHARES = (4, 4, 4, 4, 4, 4, 4, 4)
REBUILT = (1, 2)
FIRST = 1
LAG = 4
EARLY = 6
FIRST_END = 3
UNROLL = 1
EDGE_LAG = 2
VMEM_LIMIT = 6 * 2**20

acoustic = 0.4
half_acoustic = 0.5 * acoustic

f32 = jnp.float32
bf16 = jnp.bfloat16


def dot(a, b):
    return jnp.dot(a, b, preferred_element_type=f32)


def exact_dot(a, b):
    return jnp.dot(a, b, preferred_element_type=f32, precision=lax.Precision.HIGHEST)


def split(x):
    hi = x.astype(bf16)
    return hi, (x - hi.astype(f32)).astype(bf16)


def aligned(x, to):
    return x if isinstance(x, int) else pl.multiple_of(x, to)


class Plan:
    def __init__(self, groups, levels, cells, directions):
        self.groups = groups
        self.levels = levels
        self.cells = cells
        self.directions = directions
        self.total = groups * levels
        self.chunks = len(SHARES)
        self.widths = [cells * share // sum(SHARES) for share in SHARES]
        self.starts = [sum(self.widths[:c]) for c in range(self.chunks)]
        assert sum(self.widths) == cells and all(w % BLOCK == 0 for w in self.widths)
        self.extras = 1 if groups == 2 else 2
        self.rows = -(-(self.total + self.extras * groups) // 16) * 16
        self.pieces = [w // LANES for w in self.widths]
        self.sent = [(levels + self.extras) * p for p in self.pieces]
        self.slots = self.schedule()

    def schedule(self):
        chunks = self.chunks
        slots = [(0, (FIRST + q) % chunks) for q in range(chunks)]
        for substep in range(1, SUBSTEPS):
            done = {c: t + LAG for t, (s, c) in enumerate(slots) if s == substep - 1}
            ready = {}
            for c in range(chunks):
                at_edge = c in (0, chunks - 1)
                near = [done[d % chunks] + (EDGE_LAG if at_edge and not 0 <= d < chunks else 0) for d in (c - 1, c, c + 1)]
                ready[c] = (max(near), not at_edge)
            left = set(range(chunks))
            while left:
                now = [c for c in left if ready[c][0] <= len(slots)] or left
                c = min(now, key=lambda c: (ready[c][1], ready[c][0], c) if now is not left else (ready[c][0], c))
                left.remove(c)
                slots.append((substep, c))
        return slots


def operator(plan, me, inverse_ref, g_ref):
    levels, total, groups, rows = plan.levels, plan.total, plan.groups, plan.rows
    extras = plan.extras
    r = lax.broadcasted_iota(jnp.int32, (rows, total), 0)
    c = lax.broadcasted_iota(jnp.int32, (rows, total), 1)

    def wrapped(x):
        return jnp.where(x >= groups, x - groups, x)

    wanted = jnp.full((rows, total), -1, jnp.int32)
    for shift in range(groups):
        to = wrapped(me + shift)
        wanted = jnp.where((r >= shift * levels) & (r < (shift + 1) * levels), r - shift * levels + to * levels, wanted)
        first = total + shift * extras
        if groups == 2:
            edge = jnp.where(to == 0, levels, levels - 1)
            wanted = jnp.where(r == first, edge, wanted)
        else:
            wanted = jnp.where(r == first, to * levels - 1, wanted)
            wanted = jnp.where(r == first + 1, (to + 1) * levels, wanted)
    pick = (wanted == c).astype(f32)
    row = lax.broadcasted_iota(jnp.int32, (total, 2 * levels), 0)
    col = lax.broadcasted_iota(jnp.int32, (total, 2 * levels), 1)
    own = me * levels + jnp.where(col >= levels, col - levels, col)
    slope = jnp.where(row == own - 1, -half_acoustic, 0.0) + jnp.where(row == own + 1, half_acoustic, 0.0)
    mix = jnp.where(col < levels, jnp.where(row == own, 1.0, 0.0), slope)
    g = exact_dot(exact_dot(pick, inverse_ref[...]), mix)
    hi, lo = split(g)
    g_ref[0:rows, :] = hi
    g_ref[rows : 2 * rows, :] = lo


def correct(plan, me, fields, x_ref, chunk, got):
    levels, pieces = plan.levels, plan.pieces[chunk]
    row = lax.broadcasted_iota(jnp.int32, (levels, LANES), 0)
    for j in range(pieces):
        cols = pl.ds(plan.starts[chunk] + j * LANES, LANES)
        v = fields[3, :, cols]
        for g in got:
            v = v + g[j * levels : (j + 1) * levels, :]
        x = []
        for e in range(plan.extras):
            at = levels * pieces + e * pieces + j
            one = x_ref[e : e + 1, cols]
            for g in got:
                one = one + g[at : at + 1, :]
            x.append(one)
        if plan.groups == 2:
            below = jnp.where(me == 0, 0.0, x[0])
            above = jnp.where(me == 0, x[0], 0.0)
        else:
            below, above = x
        down = jnp.where(row == 0, below, pltpu.roll(v, 1, 0))
        up = jnp.where(row == levels - 1, above, pltpu.roll(v, levels - 1, 0))
        fields[2, :, cols] = fields[2, :, cols] - half_acoustic * (up - down)
        fields[3, :, cols] = v


def weights(plan, start, first, near_ref, metric_ref, m_ref, sum_ref):
    span = BLOCK + 2 * HALO
    tall = 16
    cols = pl.ds(first, BLOCK)
    directions = range(plan.directions)
    local = [near_ref[k : k + 1, cols] - (start + first) for k in directions]
    index = [jnp.broadcast_to(x, (tall, BLOCK)).astype(jnp.int16) for x in local]
    parts = []
    for which in range(2):
        w = [metric_ref[which, k : k + 1, cols] for k in directions]
        sum_ref[which : which + 1, cols] = functools.reduce(jnp.add, w)
        joined = []
        for k in directions:
            x = w[k]
            for j in range(k + 1, plan.directions):
                x = x + jnp.where(local[j] == local[k], w[j], 0.0)
            joined.append(jnp.broadcast_to(x, (tall, BLOCK)))
        pairs = [split(x) for x in joined]
        parts.append([p[0] for p in pairs])
        parts.append([p[1] for p in pairs])
    row = lax.broadcasted_iota(jnp.int32, (tall, BLOCK), 0).astype(jnp.int16)
    zero = jnp.zeros((tall, BLOCK), bf16)
    for r in range(0, span, tall):
        slot = row + jnp.int16(r)
        hits = [slot == index[k] for k in directions]
        for i, values in enumerate(parts):
            x = zero
            for k in reversed(directions):
                x = jnp.where(hits[k], values[k], x)
            m_ref[i, r : r + tall, :] = x


def advance(plan, chunk, pieces, src, origin, new, start, m, build, sum_ref, g_ref, f, x_ref, sends):
    levels, width = plan.levels, plan.widths[chunk]
    span = BLOCK + 2 * HALO
    blocks = width // BLOCK
    for ref, col, into, count in pieces:
        there = pl.ds(into, count)
        for field, places in ((0, ((1,), (0,))), (1, ((6,), (7,))), (2, ((2, 5), (3, 4)))):
            for part, rows in zip(split(ref[field, :, pl.ds(col, count)]), places):
                for at in rows:
                    f[at * levels : (at + 1) * levels, there] = part

    def block(b, carry):
        first = aligned(b * BLOCK, BLOCK)
        here = b % m.shape[0] if isinstance(b, int) else b
        if build is not None and b > 0:
            build(first, m.at[here])
        cols = pl.ds(first, BLOCK)
        mine = pl.ds(aligned(origin + first, LANES), BLOCK)
        into = pl.ds(aligned(start + first, BLOCK), BLOCK)
        wide = pl.ds(first, span)
        eh = dot(f[0 : 4 * levels, wide], m[here, 0])
        el = dot(f[levels : 3 * levels, wide], m[here, 1])
        nh = dot(f[4 * levels : 8 * levels, wide], m[here, 2])
        nl = dot(f[5 * levels : 7 * levels, wide], m[here, 3])

        def rows(x, i):
            return x[i * levels : (i + 1) * levels]

        ue = rows(eh, 0) + rows(eh, 1) + rows(el, 0)
        pe = rows(eh, 2) + rows(eh, 3) + rows(el, 1)
        pn = rows(nh, 0) + rows(nh, 1) + rows(nl, 0)
        vn = rows(nh, 2) + rows(nh, 3) + rows(nl, 1)
        se, sn = sum_ref[0:1, cols], sum_ref[1:2, cols]
        u, v, p = src[0, :, mine], src[1, :, mine], src[2, :, mine]
        new[0, :, into] = u - (pe - se * p)
        new[1, :, into] = v - (pn - sn * p)
        pressure = p - ((ue - se * u) + (vn - sn * v))
        new[2, :, into] = pressure
        z_hi, z_lo = split(jnp.concatenate([src[3, :, mine], pressure], axis=0))
        y2 = dot(g_ref[...], z_hi)
        y = y2[: plan.rows] + y2[plan.rows :] + dot(g_ref[0 : plan.rows, :], z_lo)
        new[3, :, into] = y[:levels]
        x_ref[:, into] = y[plan.total : plan.total + 8]
        for s, send in enumerate(sends):
            for i in range(BLOCK // LANES):
                part = slice(i * LANES, (i + 1) * LANES)
                j = b * (BLOCK // LANES) + i
                send[pl.ds(aligned(j * levels, 8), levels), :] = y[(s + 1) * levels : (s + 2) * levels, part]
                for e in range(plan.extras):
                    at = plan.total + (s + 1) * plan.extras + e
                    send[pl.ds((levels + e) * plan.pieces[chunk] + j, 1), :] = y[at : at + 1, part]
        return carry

    if build is None:
        lax.fori_loop(0, blocks, block, 0, unroll=UNROLL)
    else:
        for b in range(blocks):
            block(b, 0)


FAR = ("prognostic", "inverse", "near", "metric", "result")


def call(plan, arrays, outs, aliased, chunk=None, fixes=(), setup=False):
    groups, levels, cells, chunks = plan.groups, plan.levels, plan.cells, plan.chunks
    start, width = (plan.starts[chunk], plan.widths[chunk]) if chunk is not None else (0, 0)
    in_names, out_names = list(arrays), list(outs)
    fresh = "prognostic" in arrays

    scratch = {}
    if chunk is not None:
        scratch["f"] = pltpu.VMEM((8 * levels, width + 2 * HALO), bf16)
    if fresh:
        scratch["win"] = pltpu.VMEM((4, levels, width + 2 * HALO), f32)
    if "near" in arrays:
        scratch["near_v"] = pltpu.VMEM((plan.directions, width), jnp.int32)
        scratch["met_v"] = pltpu.VMEM((2, plan.directions, width), f32)
        if "m" not in outs:
            scratch["m"] = pltpu.VMEM((1, 4, BLOCK + 2 * HALO, BLOCK), bf16)
            scratch["sums"] = pltpu.VMEM((8, width), f32)
    if setup:
        scratch["inv_v"] = pltpu.VMEM((plan.total, plan.total), f32)
    scratch["sems"] = pltpu.SemaphoreType.DMA((8,))
    scratch_names = list(scratch)

    def kernel(*refs):
        r = dict(zip(in_names, refs))
        r.update(zip(out_names, refs[len(in_names) :]))
        r.update(zip(scratch_names, refs[len(in_names) + len(out_names) :]))
        used = [0]

        def copy(src, dst):
            c = pltpu.make_async_copy(src, dst, r["sems"].at[used[0]])
            used[0] += 1
            c.start()
            return c

        who = r["me"][0]
        stores = []
        loads = []
        if "near" in r:
            near = pl.ds(start, width)
            loads = [copy(r["near"].at[:, near], r["near_v"]), copy(r["metric"].at[:, :, near], r["met_v"])]
        if fresh:
            lo = start if chunk == 0 else start - HALO
            hi = start + width if chunk == chunks - 1 else start + width + HALO
            into = lo - (start - HALO)
            if setup:
                loads.append(copy(r["inverse"], r["inv_v"]))
            late = copy(r["prognostic"].at[:, :, pl.ds(lo, hi - lo)], r["win"].at[:, :, pl.ds(into, hi - lo)])
        for c in loads:
            c.wait()
        if setup:
            operator(plan, who, r["inv_v"], r["g"])
        for name, b in fixes:
            at = pl.ds(plan.starts[b], plan.widths[b])
            got = [r[f"got_{name}{b}_{s}"] for s in range(groups - 1)]
            if "result" in r:
                stores.append(copy(r[name].at[0:2, :, at], r["result"].at[0:2, :, at]))
            correct(plan, who, r[name], r[f"{name}_x"], b, got)
            if "result" in r:
                stores.append(copy(r[name].at[2:4, :, at], r["result"].at[2:4, :, at]))
            if b == 0 and "edge_low" in r:
                r["edge_low"][...] = r[name][0:3, :, 0:HALO]
            if b == chunks - 1 and "edge_high" in r:
                r["edge_high"][...] = r[name][0:3, :, cells - HALO : cells]
        if chunk is not None:
            src, origin = (r["win"], HALO) if fresh else (r["old"], start)
            lo = origin if chunk == 0 else origin - HALO
            hi = origin + width if chunk == chunks - 1 else origin + width + HALO
            pieces = [(src, lo, lo - (origin - HALO), hi - lo)]
            if chunk == 0:
                pieces.append((r["halo_low"], 0, 0, HALO))
            if chunk == chunks - 1:
                pieces.append((r["halo_high"], 0, width + HALO, HALO))
            sends = [r[f"send{s}"] for s in range(groups - 1)]
            build = None
            if "near" in r:

                def build(first, m):
                    weights(plan, start, first, r["near_v"], r["met_v"], m, r["sums"])

                build(0, r["m"].at[0])
            if fresh:
                late.wait()
            advance(
                plan, chunk, pieces, src, origin, r["new"], start, r["m"], build, r["sums"], r["g"], r["f"], r["new_x"], sends
            )
        for c in stores:
            c.wait()

    def spec(name):
        if name == "me":
            return pl.BlockSpec(memory_space=pltpu.SMEM)
        return pl.BlockSpec(memory_space=pltpu.HBM if name in FAR else pltpu.VMEM)

    def shape(name):
        s = outs[name]
        return (pltpu.HBM if name in FAR else pltpu.VMEM)(s.shape, s.dtype)

    def placed(name, x):
        if name == "me":
            return x
        return pltpu.with_memory_space_constraint(x, pltpu.HBM if name in FAR else pltpu.VMEM)

    results = pl.pallas_call(
        kernel,
        out_shape=[shape(name) for name in out_names],
        in_specs=[spec(name) for name in in_names],
        out_specs=[spec(name) for name in out_names],
        scratch_shapes=list(scratch.values()),
        input_output_aliases={in_names.index(name): out_names.index(name) for name in aliased},
        cost_estimate=pl.CostEstimate(flops=0, bytes_accessed=0, transcendentals=0),
        compiler_params=pltpu.CompilerParams(vmem_limit_bytes=VMEM_LIMIT),
        name=f"advance_{chunk}" if chunk is not None else "complete",
    )(*[placed(name, x) for name, x in arrays.items()])
    return dict(zip(out_names, results))


def per_device(prognostic, neighbours, metric, inverses):
    groups = lax.axis_size("lev")
    tiles = lax.axis_size("tile")
    levels, cells = prognostic.shape[1:]
    plan = Plan(groups, levels, cells, neighbours.shape[0])
    me = lax.axis_index("lev").astype(jnp.int32).reshape(1)

    def shape(dims, dtype=f32):
        return jax.ShapeDtypeStruct(dims, dtype)

    def shifted(x, by):
        return lax.ppermute(x, "lev", [(i, (i + by) % groups) for i in range(groups)])

    def from_low(x):
        return lax.ppermute(x, "tile", [(i, (i + 1) % tiles) for i in range(tiles)])

    def from_high(x):
        return lax.ppermute(x, "tile", [((i + 1) % tiles, i) for i in range(tiles)])

    halo_low = from_low(prognostic[0:3, :, cells - HALO :])
    halo_high = from_high(prognostic[0:3, :, :HALO])
    last = plan.chunks - 1
    state = {}
    kept, got = {}, {}
    g = result = None
    fixed = set()
    for slot in range(len(plan.slots) + LAG):
        substep, chunk = plan.slots[slot] if slot < len(plan.slots) else (SUBSTEPS - 1, None)
        due = [x for x in plan.slots[: max(slot - LAG + 1, 0)] if x not in fixed]
        if chunk is not None and substep > 0:
            due += [(substep - 1, c) for c in (chunk - 1, chunk, chunk + 1) if 0 <= c <= last and (substep - 1, c) not in fixed]
        due = list(dict.fromkeys(due))
        fixed.update(due)
        names = {substep: "new", substep - 1: "old"}
        arrays, outs, aliased = dict(me=me), {}, []
        for s in sorted({x[0] for x in due} | ({substep, substep - 1} if chunk is not None else set())):
            if s < 0:
                continue
            name = names[s]
            written = s == substep and chunk is not None
            if s in state:
                arrays[name], arrays[f"{name}_x"] = state[s]
            if written or any(x[0] == s for x in due):
                outs[name] = shape(prognostic.shape)
                if s in state:
                    aliased.append(name)
            if written:
                outs[f"{name}_x"] = shape((8, cells))
                if s in state:
                    aliased.append(f"{name}_x")
        for x in due:
            for i in range(groups - 1):
                arrays[f"got_{names[x[0]]}{x[1]}_{i}"] = got[x][i]
            if x[0] < SUBSTEPS - 1 and x[1] in (0, last):
                outs["edge_low" if x[1] == 0 else "edge_high"] = shape((3, levels, HALO))
            if x[0] == SUBSTEPS - 1 and "result" not in outs:
                outs["result"] = shape(prognostic.shape)
                if result is not None:
                    arrays["result"] = result
                    aliased.append("result")
        setup = g is None
        if chunk is not None:
            if substep == 0:
                arrays["prognostic"] = prognostic
                if chunk not in REBUILT:
                    outs["m"] = shape((plan.widths[chunk] // BLOCK, 4, BLOCK + 2 * HALO, BLOCK), dtype=bf16)
                    outs["sums"] = shape((8, plan.widths[chunk]))
            if chunk in kept:
                arrays.update(m=kept[chunk][0], sums=kept[chunk][1])
            else:
                arrays.update(near=neighbours, metric=metric)
            if slot == FIRST_END:
                for i in range(groups - 1):
                    arrays[f"first{i}"] = got[plan.slots[0]][i]
            early = slot == EARLY
            if chunk == 0 or early:
                arrays["halo_low"] = halo_low
            if chunk == last or early:
                arrays["halo_high"] = halo_high
            if setup:
                arrays["inverse"] = inverses[0]
                outs["g"] = shape((2 * plan.rows, 2 * levels), dtype=bf16)
            else:
                arrays["g"] = g
            for i in range(groups - 1):
                outs[f"send{i}"] = shape((plan.sent[chunk], LANES))
        fixes = [(names[s], c) for s, c in due]
        res = call(plan, arrays, outs, aliased, chunk=chunk, fixes=fixes, setup=setup)
        g = res.get("g", g)
        result = res.get("result", result)
        for s, name in names.items():
            if name in res:
                state[s] = res[name], res.get(f"{name}_x", state[s][1] if s in state else None)
        if chunk is not None:
            if "m" in res:
                kept[chunk] = res["m"], res["sums"]
            got[substep, chunk] = [shifted(res[f"send{i}"], i + 1) for i in range(groups - 1)]
        if "edge_high" in res:
            halo_low = from_low(res["edge_high"])
        if "edge_low" in res:
            halo_high = from_high(res["edge_low"])
    return result


def solution(mesh):
    in_specs = (
        P(None, "lev", "tile"),
        P(None, "tile"),
        P(None, None, "tile"),
        P("tile", None, None),
    )
    out_specs = P(None, "lev", "tile")
    return jax.shard_map(
        per_device, mesh=mesh, in_specs=in_specs, out_specs=out_specs, check_vma=False
    )
```
